32 devices in a mesh: dp: 2 (over core), seq: 4 (over y, x), tensor: 4 (over z).
Axes of the slice: x: 2, y: 2, z: 4, core: 2. Of those that a mesh axis runs over, the one named last changes fastest.
Arguments:
- incoming_activations: bfloat16 [2, 2048, 4096], P('dp', 'seq', 'tensor'), may hold values from -6 to 6
- objective_cotangents: bfloat16 [2, 2048, 4096], P('dp', 'seq', 'tensor'), may hold values from -400 to 400
- fixed_gating_kernel: bfloat16 [4096, 7168], P('seq', 'tensor'), may hold values from -0.09375 to 0.09375
- fixed_raising_kernel: bfloat16 [4096, 7168], P('seq', 'tensor'), may hold values from -1 to 1
- correction_narrower: bfloat16 [16, 7168], P(None, 'tensor'), may hold values from -0.0625 to 0.0625
- correction_widener: bfloat16 [16, 4096], P(None, 'tensor'), may hold values from -1.5 to 1.5
- cutoff_limits: float32 [2], replicated, may hold values from 100 to 400
Outputs:
- grad_a: float32 [16, 7168], P(None, 'tensor')
- grad_b: float32 [16, 4096], P(None, 'tensor')
The draws below stay inside these ranges and needn't reach their ends.
All inputs are finite; a program needn't handle non-finite values.
Results may differ from the reference program's by a relative error of at most 0.0041.
Values may be sent and summed in bfloat16 or wider, within the bound.
A program may use at most 128 MiB of HBM per device.

```python
import math
import jax
import jax.numpy as jnp
from jax import lax

EMBEDDING_SPAN = 4096
INNER_NEURONS = 7168
CORRECTION_ORDER = 16
LENGTH = 2048
DOCS = 2


def draw_objective_cotangents(key, part):
    first = jax.random.fold_in(key, 11)
    second = jax.random.fold_in(key, 12)
    place = jnp.arange(LENGTH, dtype=jnp.float32) / LENGTH
    base = jax.random.truncated_normal(first, -4.0, 4.0, (DOCS, LENGTH, EMBEDDING_SPAN), jnp.float32)
    row = jnp.exp(jax.random.uniform(second, (DOCS, LENGTH, 1), jnp.float32, 0.0, 2.3))
    rise = jnp.exp(place * 1.0986)[None, :, None]
    values = base * row * rise
    return values.astype(jnp.bfloat16)


def draw_fixed_raising_kernel(key, part):
    first = jax.random.fold_in(key, 21)
    scale = EMBEDDING_SPAN ** (-0.5)
    values = jax.random.truncated_normal(first, -4.0, 4.0, (EMBEDDING_SPAN, INNER_NEURONS), jnp.float32) * scale
    return values.astype(jnp.bfloat16)


def block_levels(rng, shape, split, least, largest):
    level, own = 1.0, jax.random.fold_in(rng, 6)
    for axis_at, parts in split:
        heights = jnp.exp(jax.random.uniform(jax.random.fold_in(own, axis_at), (parts,), jnp.float32, least / len(split), largest / len(split)))
        level = level * jnp.repeat(heights, shape[axis_at] // parts).reshape([-1 if axis == axis_at else 1 for axis in range(len(shape))])
    return level


def bell_draw(stream_key, shape, deviation, most, pieces=(), kind=jnp.bfloat16):
    loudness = block_levels(stream_key, shape, pieces, -0.22, 0.18) if pieces else 1.0
    values = jax.random.normal(stream_key, shape, jnp.float32) * deviation * loudness
    return jnp.minimum(jnp.maximum(values, -most), most).astype(kind)


def setup_inputs(seed: int = 0) -> dict:
    arg_keys = jax.random.split(jax.random.key(seed), 8)
    incoming_activations = bell_draw(arg_keys[0], (DOCS, LENGTH, EMBEDDING_SPAN), 1.0, 6.0, ((0, 2), (1, 4), (2, 4)))
    objective_cotangents = draw_objective_cotangents(jax.random.fold_in(arg_keys[7], 71), 0)
    fixed_gating_kernel = bell_draw(arg_keys[2], (EMBEDDING_SPAN, INNER_NEURONS), EMBEDDING_SPAN ** -0.5, 0.09375, ((0, 4), (1, 4)))
    fixed_raising_kernel = draw_fixed_raising_kernel(jax.random.fold_in(arg_keys[7], 71), 0)
    correction_narrower = bell_draw(arg_keys[4], (CORRECTION_ORDER, INNER_NEURONS), INNER_NEURONS ** -0.5, 0.0625, ((1, 4),))
    correction_widener = bell_draw(arg_keys[5], (CORRECTION_ORDER, EMBEDDING_SPAN), CORRECTION_ORDER ** -0.5, 1.5, ((1, 4),))
    cutoff_limits = jnp.clip(jnp.exp(jax.random.uniform(arg_keys[6], (2,), jnp.float32, math.log(100.0), math.log(400.0))), 100.0, 400.0)
    return {"incoming_activations": incoming_activations, "objective_cotangents": objective_cotangents, "fixed_gating_kernel": fixed_gating_kernel, "fixed_raising_kernel": fixed_raising_kernel, "correction_narrower": correction_narrower, "correction_widener": correction_widener, "cutoff_limits": cutoff_limits}


def example_contributions(example_matching, fixed_gating_kernel, fixed_raising_kernel, correction_narrower, correction_widener):
    incoming_activations, objective_cotangents = example_matching
    gate = jnp.dot(incoming_activations, fixed_gating_kernel, preferred_element_type=jnp.float32)
    up = jnp.dot(incoming_activations, fixed_raising_kernel, preferred_element_type=jnp.float32)
    inner_neurons = (jax.nn.silu(gate) * up).astype(jnp.bfloat16)
    order_quantity = jnp.dot(inner_neurons, correction_narrower.T, preferred_element_type=jnp.float32).astype(jnp.bfloat16)
    reverse_quantity = jnp.dot(objective_cotangents, correction_widener.T, preferred_element_type=jnp.float32).astype(jnp.bfloat16)
    earlier_example = jnp.dot(reverse_quantity.T, inner_neurons, preferred_element_type=jnp.float32)
    later_example = jnp.dot(order_quantity.T, objective_cotangents, preferred_element_type=jnp.float32)
    return (earlier_example, later_example)

def reference(incoming_activations, objective_cotangents, fixed_gating_kernel, fixed_raising_kernel, correction_narrower, correction_widener, cutoff_limits):
    earlier_example, later_example = lax.map(lambda example_matching: example_contributions(example_matching, fixed_gating_kernel, fixed_raising_kernel, correction_narrower, correction_widener), (incoming_activations, objective_cotangents))
    norm_a = jnp.sqrt(lax.optimization_barrier(jnp.sum(earlier_example * earlier_example, axis=(1, 2))))
    norm_b = jnp.sqrt(lax.optimization_barrier(jnp.sum(later_example * later_example, axis=(1, 2))))
    factor_a = cutoff_limits[0] / (norm_a + 0.01)
    factor_b = cutoff_limits[1] / (norm_b + 0.01)
    grad_a = lax.optimization_barrier(jnp.sum(factor_a[:, None, None] * earlier_example, axis=0))
    grad_b = lax.optimization_barrier(jnp.sum(factor_b[:, None, None] * later_example, axis=0))
    return (grad_a, grad_b)
```

```python
import functools

import jax
import jax.numpy as jnp
from jax import lax
from jax.experimental import pallas as pl
from jax.experimental.pallas import tpu as pltpu
from jax.sharding import PartitionSpec as P

F32 = jnp.float32
BF16 = jnp.bfloat16
CONTRACT_LAST = (((1,), (1,)), ((), ()))


def kernel(
    nd, ns, nt, chunks, tile,
    x_hbm, g_hbm, gate_hbm, up_hbm, narrow_hbm, widen_ref, limits_ref,
    out_a, out_b,
    xg, wbuf, acc, hid, gbuf, narrow, back_parts, low_send, low_parts,
    a_parts, b_parts, a_final, b_final, squares,
    local_sem, x_send, x_recv, w_send, w_recv, back_send, back_recv,
    lows_send, lows_recv, ab_send, ab_recv, fin_send, fin_recv, sq_send, sq_recv,
):
    d, s, t = lax.axis_index("dp"), lax.axis_index("seq"), lax.axis_index("tensor")
    rows, kx = x_hbm.shape[1:]
    kw = gate_hbm.shape[0]
    width = narrow.shape[1]
    rank = narrow.shape[0]
    kc = kw // chunks
    group = nd * nt
    mine = d * nt + t

    def at(dd, ss, tt):
        return {"dp": dd, "seq": ss, "tensor": tt}

    def remote(src, dst, ssem, rsem, where):
        return pltpu.make_async_remote_copy(
            src_ref=src, dst_ref=dst, send_sem=ssem, recv_sem=rsem,
            device_id=where, device_id_type=pl.DeviceIdType.MESH,
        )

    def peer(k):
        q = (mine + k) % group
        return q // nt, q % nt

    sent = []

    def push(*args):
        copy = remote(*args)
        copy.start()
        sent.append(copy)

    cols = pl.ds(pl.multiple_of(d * width, 128), width)
    own_rows = pl.ds(pl.multiple_of(d * rows, rows), rows)

    locals_ = [
        pltpu.make_async_copy(g_hbm.at[0], gbuf, local_sem.at[0]),
        pltpu.make_async_copy(narrow_hbm.at[:, cols], narrow, local_sem.at[1]),
        pltpu.make_async_copy(x_hbm.at[0], xg.at[t, own_rows], local_sem.at[2]),
        pltpu.make_async_copy(gate_hbm.at[:, cols], wbuf.at[s, :, pl.ds(0, width)], local_sem.at[3]),
        pltpu.make_async_copy(up_hbm.at[:, cols], wbuf.at[s, :, pl.ds(width, width)], local_sem.at[4]),
    ]
    for copy in locals_:
        copy.start()

    barrier = pltpu.get_barrier_semaphore()
    for k in range(1, group):
        dd, tt = peer(k)
        pl.semaphore_signal(barrier, inc=1, device_id=at(dd, s, tt), device_id_type=pl.DeviceIdType.MESH)
    for k in range(1, ns):
        pl.semaphore_signal(barrier, inc=1, device_id=at(d, (s + k) % ns, t), device_id_type=pl.DeviceIdType.MESH)
    pl.semaphore_wait(barrier, group - 1 + ns - 1)

    def w_slot(block, c, part):
        return wbuf.at[block, pl.ds(c * kc, kc), pl.ds(part * width, width)]

    def w_push(k, where, c):
        for part, ref in enumerate((gate_hbm, up_hbm)):
            push(ref.at[pl.ds(c * kc, kc), cols], w_slot(s, c, part), w_send.at[k, c, part],
                 w_recv.at[s, c, part], at(d, where, t))

    def w_wait(block, c):
        for part in range(2):
            slot = w_slot(block, c, part)
            remote(slot, slot, w_send.at[0, c, part], w_recv.at[block, c, part], at(d, s, t)).wait_recv()

    def w_relay(block, c, where):
        for part in range(2):
            slot = w_slot(block, c, part)
            push(slot, slot, w_send.at[2, c, part], w_recv.at[block, c, part], at(d, where, t))

    relayed = ns == 4
    half = chunks // 2
    if relayed:
        xn, yn, dg = s + 1 - 2 * (s % 2), (s + 2) % 4, 3 - s
        order = [xn, yn, dg]
        for i in range(chunks):
            w_push(0, xn, i)
            w_push(1, yn, (i + half) % chunks)
    else:
        order = [(s + k) % ns for k in range(1, ns)]
        for k, where in enumerate(order):
            for c in range(chunks):
                w_push(k, where, c)

    for k in range(1, nt):
        push(x_hbm.at[0], xg.at[t, own_rows], x_send.at[0, k], x_recv.at[t, d], at(d, s, (t + k) % nt))
    for k in range(1, nd):
        push(x_hbm.at[0], xg.at[t, own_rows], x_send.at[k, 0], x_recv.at[t, d], at((d + k) % nd, s, t))

    locals_[0].wait()
    back_parts[d, t] = lax.dot_general(widen_ref[...], gbuf[...], CONTRACT_LAST, preferred_element_type=F32)
    for k in range(1, group):
        dd, tt = peer(k)
        push(back_parts.at[d, t], back_parts.at[d, t], back_send.at[k], back_recv.at[d, t], at(dd, s, tt))

    acc[...] = jnp.zeros_like(acc)

    if relayed:
        for i in range(max(half, chunks - half)):
            if i < half:
                w_wait(xn, i)
                w_relay(xn, i, yn)
            if half + i < chunks:
                w_wait(yn, half + i)
                w_relay(yn, half + i, xn)

    def x_wait(block, doc):
        slot = xg.at[block, pl.ds(pl.multiple_of(doc * rows, rows), rows)]
        remote(slot, slot, x_send.at[0, 0], x_recv.at[block, doc], at(d, s, t)).wait_recv()

    for k in range(1, nt):
        block = (t + nt - k) % nt
        x_wait(block, d)
        for j in range(1, nd):
            push(xg.at[block, own_rows], xg.at[block, own_rows], x_send.at[j, k], x_recv.at[block, d],
                 at((d + j) % nd, s, t))
    for j in range(1, nd):
        for k in range(nt):
            x_wait((t + nt - k) % nt, (d + j) % nd)
    for copy in locals_[1:]:
        copy.wait()

    for k in range(1, group):
        dd, tt = peer(k)
        slot = back_parts.at[dd, tt]
        remote(slot, slot, back_send.at[0], back_recv.at[dd, tt], at(d, s, t)).wait_recv()
    back = [jnp.sum(back_parts[j], axis=0).astype(BF16) for j in range(nd)]

    tiles = (nd * rows) // tile

    def accumulate(block, c):
        start = block * kw + c * kc
        of, lane = start // kx, pl.multiple_of(start % kx, kc)
        w_rows = pl.ds(pl.multiple_of(c * kc, kc), kc)

        def step(i, carry):
            r = pl.ds(pl.multiple_of(i * tile, tile), tile)
            acc[r, :] += jnp.dot(xg[of, r, pl.ds(lane, kc)], wbuf[block, w_rows, :], preferred_element_type=F32)
            return carry

        lax.fori_loop(0, tiles, step, 0)

    def whole_block(block):
        def step(c, carry):
            accumulate(block, c)
            return carry

        lax.fori_loop(0, chunks, step, 0)

    whole_block(s)
    for n, block in enumerate(order):
        last = n == len(order) - 1
        if relayed and last:
            for i in range(max(half, chunks - half)):
                for c in ([i] if i < half else []) + ([half + i] if half + i < chunks else []):
                    w_wait(block, c)
                    accumulate(block, c)
        else:
            for c in range(chunks):
                if not relayed or (n == 0 and c >= half) or (n == 1 and c < half):
                    w_wait(block, c)
            whole_block(block)

    def hidden(i, carry):
        r = pl.ds(pl.multiple_of(i * tile, tile), tile)
        gate, up = acc[r, pl.ds(0, width)], acc[r, pl.ds(width, width)]
        hid[r, :] = (gate / (1.0 + jnp.exp(-gate)) * up).astype(BF16)
        return carry

    lax.fori_loop(0, tiles, hidden, 0)

    for j in range(nd):
        low_send[j] = lax.dot_general(narrow[...], hid[pl.ds(j * rows, rows), :], CONTRACT_LAST,
                                      preferred_element_type=F32)
    for k in range(1, group):
        dd, tt = peer(k)
        push(low_send.at[dd], low_parts.at[d, t], lows_send.at[k], lows_recv.at[d, t], at(dd, s, tt))
    low_parts[d, t] = low_send[d]

    def ab_push(parts, which):
        for k in range(1, ns):
            push(parts.at[s], parts.at[s], ab_send.at[which, k], ab_recv.at[which, s], at(d, (s + k) % ns, t))

    def ab_wait(parts, which):
        for k in range(1, ns):
            slot = parts.at[(s + k) % ns]
            remote(slot, slot, ab_send.at[which, 0], ab_recv.at[which, (s + k) % ns], at(d, s, t)).wait_recv()

    for j in range(nd):
        a_parts[s, pl.ds(j * rank, rank), :] = jnp.dot(
            back[j], hid[pl.ds(j * rows, rows), :], preferred_element_type=F32)
    ab_push(a_parts, 0)

    for k in range(1, group):
        dd, tt = peer(k)
        slot = low_parts.at[dd, tt]
        remote(slot, slot, lows_send.at[0], lows_recv.at[dd, tt], at(d, s, t)).wait_recv()
    low = jnp.sum(low_parts[...], axis=(0, 1)).astype(BF16)
    b_parts[s] = jnp.dot(low, gbuf[...], preferred_element_type=F32)
    ab_push(b_parts, 1)

    ab_wait(a_parts, 0)
    doc_a = jnp.sum(a_parts[...], axis=0)
    a_final[d] = doc_a

    def fin_push(ref, which):
        for k in range(1, nd):
            push(ref.at[d], ref.at[d], fin_send.at[which, k], fin_recv.at[which, d], at((d + k) % nd, s, t))

    def fin_wait(ref, which):
        for k in range(1, nd):
            slot = ref.at[(d + k) % nd]
            remote(slot, slot, fin_send.at[which, 0], fin_recv.at[which, (d + k) % nd], at(d, s, t)).wait_recv()

    fin_push(a_final, 0)
    ab_wait(b_parts, 1)
    doc_b = jnp.sum(b_parts[...], axis=0)
    b_final[d] = doc_b
    fin_push(b_final, 1)

    def total(v):
        return jnp.sum(jnp.sum(v * v, axis=0, keepdims=True), axis=1, keepdims=True)

    line = lax.broadcasted_iota(jnp.int32, squares.shape[2:], 0)
    own = jnp.where(line == nd, total(doc_b), 0.0)
    for j in range(nd):
        own = jnp.where(line == j, total(doc_a[j * rank:(j + 1) * rank]), own)
    squares[d, t] = own
    for k in range(1, group):
        dd, tt = peer(k)
        push(squares.at[d, t], squares.at[d, t], sq_send.at[k], sq_recv.at[d, t], at(dd, s, tt))
    for k in range(1, group):
        dd, tt = peer(k)
        slot = squares.at[dd, tt]
        remote(slot, slot, sq_send.at[0], sq_recv.at[dd, tt], at(d, s, t)).wait_recv()
    per_doc = jnp.sum(squares[...], axis=1)
    over_docs = jnp.sum(per_doc, axis=0)

    fin_wait(a_final, 0)
    fin_wait(b_final, 1)
    factor_a = [limits_ref[0] / (jnp.sqrt(over_docs[j:j + 1, 0:1]) + 0.01) for j in range(nd)]
    factor_b = [limits_ref[1] / (jnp.sqrt(per_doc[j, nd:nd + 1, 0:1]) + 0.01) for j in range(nd)]
    for part in range(nd):
        out_a[:, pl.ds(part * width, width)] = sum(
            factor_a[j] * a_final[part, pl.ds(j * rank, rank), :] for j in range(nd))
    out_b[...] = sum(factor_b[j] * b_final[j] for j in range(nd))

    for copy in sent:
        copy.wait_send()


def body(x, g, gate, up, narrower, widener, limits):
    nd, ns, nt = lax.axis_size("dp"), lax.axis_size("seq"), lax.axis_size("tensor")
    rows, kx = x.shape[1:]
    kw, full = gate.shape
    rank = narrower.shape[0]
    width = full // nd
    kc = min(kw, 256)
    chunks = kw // kc
    dma = pltpu.SemaphoreType.DMA
    lines = -(-(nd + 1) // 8) * 8
    any_, vmem, smem = (pl.BlockSpec(memory_space=m) for m in (pl.ANY, pltpu.VMEM, pltpu.SMEM))
    return pl.pallas_call(
        functools.partial(kernel, nd, ns, nt, chunks, 256),
        out_shape=(
            jax.ShapeDtypeStruct((rank, full), F32),
            jax.ShapeDtypeStruct((rank, kx), F32),
        ),
        in_specs=[any_] * 5 + [vmem, smem],
        out_specs=(vmem, vmem),
        scratch_shapes=[
            pltpu.VMEM((nt, nd * rows, kx), BF16),
            pltpu.VMEM((ns, kw, 2 * width), BF16),
            pltpu.VMEM((nd * rows, 2 * width), F32),
            pltpu.VMEM((nd * rows, width), BF16),
            pltpu.VMEM((rows, kx), BF16),
            pltpu.VMEM((rank, width), BF16),
            pltpu.VMEM((nd, nt, rank, rows), F32),
            pltpu.VMEM((nd, rank, rows), F32),
            pltpu.VMEM((nd, nt, rank, rows), F32),
            pltpu.VMEM((ns, nd * rank, width), F32),
            pltpu.VMEM((ns, rank, kx), F32),
            pltpu.VMEM((nd, nd * rank, width), F32),
            pltpu.VMEM((nd, rank, kx), F32),
            pltpu.VMEM((nd, nt, lines, 128), F32),
            dma((5,)),
            dma((nd, nt)), dma((nt, nd)),
            dma((max(ns - 1, 3), chunks, 2)), dma((ns, chunks, 2)),
            dma((nd * nt,)), dma((nd, nt)),
            dma((nd * nt,)), dma((nd, nt)),
            dma((2, ns)), dma((2, ns)),
            dma((2, nd)), dma((2, nd)),
            dma((nd * nt,)), dma((nd, nt)),
        ],
        compiler_params=pltpu.CompilerParams(
            collective_id=0, has_side_effects=True, vmem_limit_bytes=56 * 2**20),
        name="adapter_gradients",
    )(x, g, gate, up, narrower, widener, limits)


def solution(mesh):
    in_specs = (
        P("dp", "seq", "tensor"),
        P("dp", "seq", "tensor"),
        P("seq", "tensor"),
        P("seq", "tensor"),
        P(None, "tensor"),
        P(None, "tensor"),
        P(),
    )
    out_specs = (P(None, "tensor"), P(None, "tensor"))
    return jax.shard_map(body, mesh=mesh, in_specs=in_specs, out_specs=out_specs, check_vma=False)
```

```python
import functools

import jax
import jax.numpy as jnp
from jax import lax
from jax.experimental import pallas as pl
from jax.experimental.pallas import tpu as pltpu
from jax.sharding import PartitionSpec as P

F32 = jnp.float32
BF16 = jnp.bfloat16
CONTRACT_LAST = (((1,), (1,)), ((), ()))


def kernel(
    nd, ns, nt, chunks, tile,
    x_hbm, g_hbm, gate_hbm, up_hbm, narrow_hbm, widen_ref, limits_ref,
    out_a, out_b,
    xg, wbuf, acc, hid, gbuf, narrow, back_parts, low_send, low_parts,
    a_parts, b_parts, a_final, b_final, squares,
    local_sem, x_send, x_recv, w_send, w_recv, back_send, back_recv,
    lows_send, lows_recv, ab_send, ab_recv, fin_send, fin_recv, sq_send, sq_recv,
):
    d, s, t = lax.axis_index("dp"), lax.axis_index("seq"), lax.axis_index("tensor")
    rows, kx = x_hbm.shape[1:]
    kw = gate_hbm.shape[0]
    width = narrow.shape[1]
    rank = narrow.shape[0]
    kc = kw // chunks
    group = nd * nt
    mine = d * nt + t

    def at(dd, ss, tt):
        return {"dp": dd, "seq": ss, "tensor": tt}

    def remote(src, dst, ssem, rsem, where):
        return pltpu.make_async_remote_copy(
            src_ref=src, dst_ref=dst, send_sem=ssem, recv_sem=rsem,
            device_id=where, device_id_type=pl.DeviceIdType.MESH,
        )

    def peer(k):
        q = (mine + k) % group
        return q // nt, q % nt

    sent = []

    def push(*args):
        copy = remote(*args)
        copy.start()
        sent.append(copy)

    cols = pl.ds(pl.multiple_of(d * width, 128), width)
    own_rows = pl.ds(pl.multiple_of(d * rows, rows), rows)

    locals_ = [
        pltpu.make_async_copy(g_hbm.at[0], gbuf, local_sem.at[0]),
        pltpu.make_async_copy(narrow_hbm.at[:, cols], narrow, local_sem.at[1]),
        pltpu.make_async_copy(x_hbm.at[0], xg.at[t, own_rows], local_sem.at[2]),
        pltpu.make_async_copy(gate_hbm.at[:, cols], wbuf.at[s, :, pl.ds(0, width)], local_sem.at[3]),
        pltpu.make_async_copy(up_hbm.at[:, cols], wbuf.at[s, :, pl.ds(width, width)], local_sem.at[4]),
    ]
    for copy in locals_:
        copy.start()

    barrier = pltpu.get_barrier_semaphore()
    for k in range(1, group):
        dd, tt = peer(k)
        pl.semaphore_signal(barrier, inc=1, device_id=at(dd, s, tt), device_id_type=pl.DeviceIdType.MESH)
    for k in range(1, ns):
        pl.semaphore_signal(barrier, inc=1, device_id=at(d, (s + k) % ns, t), device_id_type=pl.DeviceIdType.MESH)
    pl.semaphore_wait(barrier, group - 1 + ns - 1)

    def w_slot(block, c, part):
        return wbuf.at[block, pl.ds(c * kc, kc), pl.ds(part * width, width)]

    def w_push(k, where, c):
        for part, ref in enumerate((gate_hbm, up_hbm)):
            push(ref.at[pl.ds(c * kc, kc), cols], w_slot(s, c, part), w_send.at[k, c, part],
                 w_recv.at[s, c, part], at(d, where, t))

    def w_wait(block, c):
        for part in range(2):
            slot = w_slot(block, c, part)
            remote(slot, slot, w_send.at[0, c, part], w_recv.at[block, c, part], at(d, s, t)).wait_recv()

    def w_relay(block, c, where):
        for part in range(2):
            slot = w_slot(block, c, part)
            push(slot, slot, w_send.at[2, c, part], w_recv.at[block, c, part], at(d, where, t))

    relayed = ns == 4
    half = chunks // 2
    if relayed:
        xn, yn, dg = s + 1 - 2 * (s % 2), (s + 2) % 4, 3 - s
        order = [xn, yn, dg]
        for i in range(chunks):
            w_push(0, xn, i)
            w_push(1, yn, (i + half) % chunks)
    else:
        order = [(s + k) % ns for k in range(1, ns)]
        for k, where in enumerate(order):
            for c in range(chunks):
                w_push(k, where, c)

    for k in range(1, nt):
        push(x_hbm.at[0], xg.at[t, own_rows], x_send.at[0, k], x_recv.at[t, d], at(d, s, (t + k) % nt))
    for k in range(1, nd):
        push(x_hbm.at[0], xg.at[t, own_rows], x_send.at[k, 0], x_recv.at[t, d], at((d + k) % nd, s, t))

    locals_[0].wait()
    back_parts[d, t] = lax.dot_general(widen_ref[...], gbuf[...], CONTRACT_LAST, preferred_element_type=F32)
    for k in range(1, group):
        dd, tt = peer(k)
        push(back_parts.at[d, t], back_parts.at[d, t], back_send.at[k], back_recv.at[d, t], at(dd, s, tt))

    acc[...] = jnp.zeros_like(acc)

    if relayed:
        for i in range(max(half, chunks - half)):
            if i < half:
                w_wait(xn, i)
                w_relay(xn, i, yn)
            if half + i < chunks:
                w_wait(yn, half + i)
                w_relay(yn, half + i, xn)

    def x_wait(block, doc):
        slot = xg.at[block, pl.ds(pl.multiple_of(doc * rows, rows), rows)]
        remote(slot, slot, x_send.at[0, 0], x_recv.at[block, doc], at(d, s, t)).wait_recv()

    for k in range(1, nt):
        block = (t + nt - k) % nt
        x_wait(block, d)
        for j in range(1, nd):
            push(xg.at[block, own_rows], xg.at[block, own_rows], x_send.at[j, k], x_recv.at[block, d],
                 at((d + j) % nd, s, t))
    for j in range(1, nd):
        for k in range(nt):
            x_wait((t + nt - k) % nt, (d + j) % nd)
    for copy in locals_[1:]:
        copy.wait()

    for k in range(1, group):
        dd, tt = peer(k)
        slot = back_parts.at[dd, tt]
        remote(slot, slot, back_send.at[0], back_recv.at[dd, tt], at(d, s, t)).wait_recv()
    back = [jnp.sum(back_parts[j], axis=0).astype(BF16) for j in range(nd)]

    tiles = (nd * rows) // tile

    def accumulate(block, c):
        start = block * kw + c * kc
        of, lane = start // kx, pl.multiple_of(start % kx, kc)
        w_rows = pl.ds(pl.multiple_of(c * kc, kc), kc)

        def step(i, carry):
            r = pl.ds(pl.multiple_of(i * tile, tile), tile)
            acc[r, :] += jnp.dot(xg[of, r, pl.ds(lane, kc)], wbuf[block, w_rows, :], preferred_element_type=F32)
            return carry

        lax.fori_loop(0, tiles, step, 0)

    def whole_block(block):
        def step(c, carry):
            accumulate(block, c)
            return carry

        lax.fori_loop(0, chunks, step, 0)

    whole_block(s)
    for n, block in enumerate(order):
        last = n == len(order) - 1
        if relayed and last:
            for i in range(max(half, chunks - half)):
                for c in ([i] if i < half else []) + ([half + i] if half + i < chunks else []):
                    w_wait(block, c)
                    accumulate(block, c)
        else:
            for c in range(chunks):
                if not relayed or (n == 0 and c >= half) or (n == 1 and c < half):
                    w_wait(block, c)
            whole_block(block)

    def hidden(i, carry):
        r = pl.ds(pl.multiple_of(i * tile, tile), tile)
        gate, up = acc[r, pl.ds(0, width)], acc[r, pl.ds(width, width)]
        hid[r, :] = (gate / (1.0 + jnp.exp(-gate)) * up).astype(BF16)
        return carry

    lax.fori_loop(0, tiles, hidden, 0)

    for j in range(nd):
        low_send[j] = lax.dot_general(narrow[...], hid[pl.ds(j * rows, rows), :], CONTRACT_LAST,
                                      preferred_element_type=F32)
    for k in range(1, group):
        dd, tt = peer(k)
        push(low_send.at[dd], low_parts.at[d, t], lows_send.at[k], lows_recv.at[d, t], at(dd, s, tt))
    low_parts[d, t] = low_send[d]

    def ab_push(parts, which):
        for k in range(1, ns):
            push(parts.at[s], parts.at[s], ab_send.at[which, k], ab_recv.at[which, s], at(d, (s + k) % ns, t))

    def ab_wait(parts, which):
        for k in range(1, ns):
            slot = parts.at[(s + k) % ns]
            remote(slot, slot, ab_send.at[which, 0], ab_recv.at[which, (s + k) % ns], at(d, s, t)).wait_recv()

    for j in range(nd):
        a_parts[s, pl.ds(j * rank, rank), :] = jnp.dot(
            back[j], hid[pl.ds(j * rows, rows), :], preferred_element_type=F32)
    ab_push(a_parts, 0)

    for k in range(1, group):
        dd, tt = peer(k)
        slot = low_parts.at[dd, tt]
        remote(slot, slot, lows_send.at[0], lows_recv.at[dd, tt], at(d, s, t)).wait_recv()
    low = jnp.sum(low_parts[...], axis=(0, 1)).astype(BF16)
    b_parts[s] = jnp.dot(low, gbuf[...], preferred_element_type=F32)
    ab_push(b_parts, 1)

    ab_wait(a_parts, 0)
    doc_a = jnp.sum(a_parts[...], axis=0)
    a_final[d] = doc_a

    def fin_push(ref, which):
        for k in range(1, nd):
            push(ref.at[d], ref.at[d], fin_send.at[which, k], fin_recv.at[which, d], at((d + k) % nd, s, t))

    def fin_wait(ref, which):
        for k in range(1, nd):
            slot = ref.at[(d + k) % nd]
            remote(slot, slot, fin_send.at[which, 0], fin_recv.at[which, (d + k) % nd], at(d, s, t)).wait_recv()

    fin_push(a_final, 0)
    ab_wait(b_parts, 1)
    doc_b = jnp.sum(b_parts[...], axis=0)
    b_final[d] = doc_b
    fin_push(b_final, 1)

    def total(v):
        return jnp.sum(jnp.sum(v * v, axis=0, keepdims=True), axis=1, keepdims=True)

    line = lax.broadcasted_iota(jnp.int32, squares.shape[2:], 0)
    own = jnp.where(line == nd, total(doc_b), 0.0)
    for j in range(nd):
        own = jnp.where(line == j, total(doc_a[j * rank:(j + 1) * rank]), own)
    squares[d, t] = own
    for k in range(1, group):
        dd, tt = peer(k)
        push(squares.at[d, t], squares.at[d, t], sq_send.at[k], sq_recv.at[d, t], at(dd, s, tt))
    for k in range(1, group):
        dd, tt = peer(k)
        slot = squares.at[dd, tt]
        remote(slot, slot, sq_send.at[0], sq_recv.at[dd, tt], at(d, s, t)).wait_recv()
    per_doc = jnp.sum(squares[...], axis=1)
    over_docs = jnp.sum(per_doc, axis=0)

    fin_wait(a_final, 0)
    fin_wait(b_final, 1)
    factor_a = [limits_ref[0] / (jnp.sqrt(over_docs[j:j + 1, 0:1]) + 0.01) for j in range(nd)]
    factor_b = [limits_ref[1] / (jnp.sqrt(per_doc[j, nd:nd + 1, 0:1]) + 0.01) for j in range(nd)]
    for part in range(nd):
        out_a[:, pl.ds(part * width, width)] = sum(
            factor_a[j] * a_final[part, pl.ds(j * rank, rank), :] for j in range(nd))
    out_b[...] = sum(factor_b[j] * b_final[j] for j in range(nd))

    for copy in sent:
        copy.wait_send()


def body(x, g, gate, up, narrower, widener, limits):
    nd, ns, nt = lax.axis_size("dp"), lax.axis_size("seq"), lax.axis_size("tensor")
    rows, kx = x.shape[1:]
    kw, full = gate.shape
    rank = narrower.shape[0]
    width = full // nd
    kc = min(kw, 512)
    chunks = kw // kc
    dma = pltpu.SemaphoreType.DMA
    lines = -(-(nd + 1) // 8) * 8
    any_, vmem, smem = (pl.BlockSpec(memory_space=m) for m in (pl.ANY, pltpu.VMEM, pltpu.SMEM))
    return pl.pallas_call(
        functools.partial(kernel, nd, ns, nt, chunks, 256),
        out_shape=(
            jax.ShapeDtypeStruct((rank, full), F32),
            jax.ShapeDtypeStruct((rank, kx), F32),
        ),
        in_specs=[any_] * 5 + [vmem, smem],
        out_specs=(vmem, vmem),
        scratch_shapes=[
            pltpu.VMEM((nt, nd * rows, kx), BF16),
            pltpu.VMEM((ns, kw, 2 * width), BF16),
            pltpu.VMEM((nd * rows, 2 * width), F32),
            pltpu.VMEM((nd * rows, width), BF16),
            pltpu.VMEM((rows, kx), BF16),
            pltpu.VMEM((rank, width), BF16),
            pltpu.VMEM((nd, nt, rank, rows), F32),
            pltpu.VMEM((nd, rank, rows), F32),
            pltpu.VMEM((nd, nt, rank, rows), F32),
            pltpu.VMEM((ns, nd * rank, width), F32),
            pltpu.VMEM((ns, rank, kx), F32),
            pltpu.VMEM((nd, nd * rank, width), F32),
            pltpu.VMEM((nd, rank, kx), F32),
            pltpu.VMEM((nd, nt, lines, 128), F32),
            dma((5,)),
            dma((nd, nt)), dma((nt, nd)),
            dma((max(ns - 1, 3), chunks, 2)), dma((ns, chunks, 2)),
            dma((nd * nt,)), dma((nd, nt)),
            dma((nd * nt,)), dma((nd, nt)),
            dma((2, ns)), dma((2, ns)),
            dma((2, nd)), dma((2, nd)),
            dma((nd * nt,)), dma((nd, nt)),
        ],
        compiler_params=pltpu.CompilerParams(
            collective_id=0, has_side_effects=True, vmem_limit_bytes=56 * 2**20),
        name="adapter_gradients",
    )(x, g, gate, up, narrower, widener, limits)


def solution(mesh):
    in_specs = (
        P("dp", "seq", "tensor"),
        P("dp", "seq", "tensor"),
        P("seq", "tensor"),
        P("seq", "tensor"),
        P(None, "tensor"),
        P(None, "tensor"),
        P(),
    )
    out_specs = (P(None, "tensor"), P(None, "tensor"))
    return jax.shard_map(body, mesh=mesh, in_specs=in_specs, out_specs=out_specs, check_vma=False)
```
